512 devices in a mesh: dp: 32 (over z_lo, y, core), seq: 16 (over x, z_hi).
Axes of the slice: x: 4, y: 4, z: 16 (z_hi: 4, z_lo: 4; z = z_hi * 4 + z_lo), core: 2. Of those that a mesh axis runs over, the one named last changes fastest.
Arguments:
- out_gate: bfloat16 [32, 2048, 2048], P('dp', 'seq'), may hold values from -6 to 6
- in_gate: bfloat16 [32, 2048, 2048], P('dp', 'seq'), may hold values from -6 to 6
- signal: bfloat16 [32, 2048, 2048], P('dp', 'seq'), may hold values from -6 to 6
- upstream: bfloat16 [32, 2048, 2048], P('dp', 'seq'), may hold values from -6 to 6
- filter_taps: bfloat16 [2048, 2048], P('seq'), may hold values from -0.75 to 0.75
- skip_gain: float32 [2048], replicated, may hold values from -1 to 1
Outputs:
- grad_in_gate: bfloat16 [32, 2048, 2048], P('dp', 'seq')
- grad_signal: bfloat16 [32, 2048, 2048], P('dp', 'seq')
- grad_filter: float32 [2048, 2048], P('dp', 'seq')
The draws below stay inside these ranges and needn't reach their ends.
All inputs are finite; a program needn't handle non-finite values.
Results may differ from the reference program's by a relative error of at most 0.008.
Values may be sent and summed in bfloat16 or wider, within the bound.
A program may use at most 128 MiB of HBM per device.

```python
import math
import jax
import jax.numpy as jnp
from jax import lax

CHANNELS = 2048
LENGTH = 2048
SEQS = 32


def draw_filter_taps(key, part):
    key = jax.random.fold_in(key, 7)
    rate_key, jitter_key = jax.random.split(key)
    lower_end = math.log(30.0)
    upper_end = math.log(2.0 * LENGTH)
    jitter = jax.random.truncated_normal(jitter_key, -4.0, 4.0, (LENGTH, CHANNELS), jnp.float32)
    lifetimes = jnp.exp(jax.random.uniform(rate_key, (CHANNELS,), jnp.float32, lower_end, upper_end))
    positions = jnp.arange(LENGTH, dtype=jnp.float32)[:, None]
    amplitude = 1.0 / jnp.sqrt(jnp.minimum(lifetimes, LENGTH * 1.0))
    return (jitter * jnp.exp(-positions / lifetimes[None, :]) * amplitude[None, :]).astype(jnp.bfloat16)


def shard_levels(stream_key, dims, cuts, low, largest):
    factor_of, own = 1.0, jax.random.fold_in(stream_key, 6)
    for dim, blocks in cuts:
        draws = jnp.exp(jax.random.uniform(jax.random.fold_in(own, dim), (blocks,), jnp.float32, low / len(cuts), largest / len(cuts)))
        factor_of = factor_of * jnp.repeat(draws, dims[dim] // blocks).reshape([-1 if axis == dim else 1 for axis in range(len(dims))])
    return factor_of


def noise(own_key, dims, scale, reach, shards=(), kind=jnp.bfloat16):
    array = scale * jax.random.normal(own_key, dims, jnp.float32)
    if shards:
        array = array * shard_levels(own_key, dims, shards, -0.22, 0.18)
    return jnp.clip(array, -reach, reach).astype(kind)


def setup_inputs(seed: int = 0) -> dict:
    key_list = jax.random.split(jax.random.key(seed), 7)
    return {
        "out_gate": noise(key_list[0], (SEQS, LENGTH, CHANNELS), 1.0, 6.0, ((0, 32), (1, 16))),
        "in_gate": noise(key_list[1], (SEQS, LENGTH, CHANNELS), 1.0, 6.0, ((0, 32), (1, 16))),
        "signal": noise(key_list[2], (SEQS, LENGTH, CHANNELS), 1.0, 6.0, ((0, 32), (1, 16))),
        "upstream": noise(key_list[3], (SEQS, LENGTH, CHANNELS), 1.0, 6.0, ((0, 32), (1, 16))),
        "filter_taps": draw_filter_taps(jax.random.fold_in(key_list[6], 71), 0),
        "skip_gain": jnp.clip(jax.random.uniform(key_list[5], (CHANNELS,), jnp.float32, -1.0, 1.0), -1.0, 1.0),
    }


def reference(out_gate, in_gate, signal, upstream, filter_taps, skip_gain):
    span_all = 2 * LENGTH
    taps_spec = jnp.fft.rfft(filter_taps.astype(jnp.float32), n=span_all, axis=0)

    def one_sequence(lag_total, inputs):
        gate_out, gate_in, values_in, grad_out = inputs
        gated_grad = (grad_out.astype(jnp.float32) * gate_out.astype(jnp.float32)).astype(jnp.bfloat16)
        conv_input = (gate_in.astype(jnp.float32) * values_in.astype(jnp.float32)).astype(jnp.bfloat16)
        grad_spec = jnp.fft.rfft(gated_grad.astype(jnp.float32), n=span_all, axis=0)
        input_spec = jnp.fft.rfft(conv_input.astype(jnp.float32), n=span_all, axis=0)
        back_conv = jnp.fft.irfft(jnp.conj(taps_spec) * grad_spec, n=span_all, axis=0)[:LENGTH].astype(jnp.bfloat16)
        lag_terms = jnp.fft.irfft(grad_spec * jnp.conj(input_spec), n=span_all, axis=0)[:LENGTH]
        input_grad = back_conv.astype(jnp.float32) + skip_gain.astype(jnp.float32)[None, :] * gated_grad.astype(jnp.float32)
        grad_gate = (input_grad * values_in.astype(jnp.float32)).astype(jnp.bfloat16)
        grad_values = (input_grad * gate_in.astype(jnp.float32)).astype(jnp.bfloat16)
        return lag_total + lag_terms.astype(jnp.float32), (grad_gate, grad_values)

    lag_total, outputs = lax.scan(one_sequence, jnp.zeros((LENGTH, CHANNELS), jnp.float32),
                                  (out_gate, in_gate, signal, upstream))
    return outputs[0], outputs[1], lag_total / SEQS
```

```python
import jax
import jax.numpy as jnp
from jax import lax
from jax.experimental import pallas as pl
from jax.experimental.pallas import tpu as pltpu
from jax.sharding import PartitionSpec as P

MESH = pl.DeviceIdType.MESH
f32 = jnp.float32
bf16 = jnp.bfloat16

Z_ORDER = (2, 1, 3, 0)
SEQ_OFFS = [(dx, dz) for dz in Z_ORDER for dx in range(4) if (dx, dz) != (0, 0)]
SEQ_SLOT = {off: i for i, off in enumerate(SEQ_OFFS)}


def kernel(
    og, ig, sg, up, ft, skip,
    oa, ob, of,
    gT, uT, hT, g1, u1, H, G, U, BC, R1, bT, Gf, Uf, Bf, HR, Lp, L, LZ, LS, LQ,
    g1s, g1r, u1s, u1r, hs, hr, g2s, g2r, u2s, u2r, b2s, b2r, b1s, b1r, lzs, lzr, lqs, lqr,
):
    dp = lax.axis_index("dp")
    sq = lax.axis_index("seq")
    x, zh = sq // 4, sq % 4
    zl, q = dp // 8, dp % 8

    def seq_index(dx, dz, sign):
        return ((x + sign * dx + 4) % 4) * 4 + (zh + sign * dz + 4) % 4

    def seq_dev(dx, dz, sign=1):
        return (dp, seq_index(dx, dz, sign))

    def q_index(k, sign=1):
        return (q + sign * k + 8) % 8

    def q_dev(k, sign=1):
        return (zl * 8 + q_index(k, sign), sq)

    def zl_index(k, sign=1):
        return (zl + sign * k + 4) % 4

    def zl_dev(k, sign=1):
        return (zl_index(k, sign) * 8 + q, sq)

    def remote(src, dst, ssem, rsem, dev):
        return pltpu.make_async_remote_copy(
            src_ref=src, dst_ref=dst, send_sem=ssem, recv_sem=rsem,
            device_id=dev, device_id_type=MESH,
        )

    barrier = pltpu.get_barrier_semaphore()
    for dx, dz in SEQ_OFFS:
        pl.semaphore_signal(barrier, inc=1, device_id=seq_dev(dx, dz), device_id_type=MESH)
    for k in range(1, 8):
        pl.semaphore_signal(barrier, inc=1, device_id=q_dev(k), device_id_type=MESH)
    for k in range(1, 4):
        pl.semaphore_signal(barrier, inc=1, device_id=zl_dev(k), device_id_type=MESH)

    def gated(a_ref, b_ref, cols):
        return (a_ref[:, cols].astype(f32) * b_ref[:, cols].astype(f32)).astype(bf16)

    def prepare(a_ref, b_ref, out):
        def body(k, carry):
            cols = pl.ds(pl.multiple_of(k * 128, 128), 128)
            out[k] = gated(a_ref, b_ref, cols).astype(f32).T.astype(bf16)
            return carry
        lax.fori_loop(0, 16, body, 0)

    prepare(up, og, gT)

    pl.semaphore_wait(barrier, 25)

    def scatter(send, recv, ss, rs):
        copies = {}
        for i, (dx, dz) in enumerate(SEQ_OFFS):
            t = seq_index(dx, dz, 1)
            c = remote(send.at[t], recv.at[x, zh], ss.at[i], rs.at[i], seq_dev(dx, dz))
            c.start()
            copies[(dx, dz)] = c
        return copies

    cg = scatter(gT, g1, g1s, g1r)

    def hbody(k, carry):
        cols = pl.ds(pl.multiple_of(k * 128, 128), 128)
        hT[k] = ft[:, cols].astype(f32).T.astype(bf16)
        return carry
    lax.fori_loop(0, 16, hbody, 0)
    mine = pl.ds(pl.multiple_of(q * 16, 16), 16)
    ch = []
    for i, (dx, dz) in enumerate(SEQ_OFFS):
        t = seq_index(dx, dz, 1)
        c = remote(hT.at[t, mine], H.at[sq], hs.at[i], hr.at[i], seq_dev(dx, dz))
        c.start()
        ch.append(c)
    H[sq] = hT[sq, mine, :]

    prepare(ig, sg, uT)
    cu = scatter(uT, u1, u1s, u1r)
    g1[x, zh] = gT[sq]
    u1[x, zh] = uT[sq]

    def spread(first, cs, stage, out, ss, rs):
        copies = []
        for n, dz in enumerate(Z_ORDER):
            for dx in range(4):
                if (dx, dz) != (0, 0):
                    cs[(dx, dz)].wait_recv()
            zsrc = (zh - dz + 4) % 4
            for k in range(1, 8):
                t = pl.ds(pl.multiple_of(q_index(k) * 16, 16), 16)
                c = remote(
                    first.at[:, zsrc, t, :], out.at[:, zsrc, q],
                    ss.at[n, k - 1], rs.at[n, k - 1], q_dev(k),
                )
                c.start()
                copies.append(c)
            out[:, zsrc, q] = first[:, zsrc, mine, :]
        return copies

    cg2 = spread(g1, cg, 0, G, g2s, g2r)

    row = lax.broadcasted_iota(jnp.int32, (128, 128), 0)
    col = lax.broadcasted_iota(jnp.int32, (128, 128), 1)
    lower = col <= row
    flip = jnp.where(row + col == 127, 1.0, 0.0).astype(bf16)

    for c in ch:
        c.wait_recv()
    HR[...] = jnp.dot(H[...].reshape(256, 128), flip, preferred_element_type=f32)

    for c in cg2:
        c.wait_recv()
    Gf[...] = G[...].reshape(2048, 128).astype(f32)

    def shifted(c):
        rows = Gf[pl.ds(c, 128, stride=16), :]
        zero = jnp.zeros((128, 128), f32)
        even = jnp.concatenate([rows, zero], 0).astype(bf16)
        odd = jnp.concatenate([rows[8:], zero, zero[:8]], 0).astype(bf16)
        return [(even, odd)[d % 2][(d // 2) * 16:(d // 2) * 16 + 128] for d in range(16)]

    def conv_body(c, carry):
        gs = shifted(c)
        h = HR[pl.ds(c, 16, stride=16), :]
        prev = jnp.zeros((128, 128), f32)
        total = jnp.zeros((128, 128), f32)
        for e in range(8):
            ws = []
            for d in (2 * e, 2 * e + 1):
                rolled = pltpu.roll(
                    jnp.broadcast_to(h[d:d + 1], (128, 128)), 1, 1, stride=1, stride_axis=0
                )
                ws.append(jnp.where(lower, rolled, prev).astype(bf16))
                prev = rolled
            total += jnp.dot(
                jnp.concatenate([gs[2 * e], gs[2 * e + 1]], 1), jnp.concatenate(ws, 0),
                preferred_element_type=f32,
            )
        Bf[pl.ds(c, 128, stride=16), :] = total
        return carry
    lax.fori_loop(0, 16, conv_body, 0)
    BC[...] = Bf[...].astype(bf16).reshape(4, 4, 8, 16, 128)

    cb2 = []
    for n, dz in enumerate(Z_ORDER):
        zt = (zh + dz) % 4
        group = []
        for k in range(1, 8):
            c = remote(
                BC.at[:, zt, q_index(k)], R1.at[:, zt, mine, :],
                b2s.at[n, k - 1], b2r.at[n, k - 1], q_dev(k),
            )
            c.start()
            group.append(c)
        R1[:, zt, mine, :] = BC[:, zt, q]
        cb2.append(group)
    cb1 = {}
    for n, dz in enumerate(Z_ORDER):
        for c in cb2[n]:
            c.wait_recv()
        zt = (zh + dz) % 4
        for dx in range(4):
            if (dx, dz) == (0, 0):
                continue
            i = SEQ_SLOT[(dx, dz)]
            c = remote(
                R1.at[(x + dx) % 4, zt], bT.at[sq], b1s.at[i], b1r.at[i], seq_dev(dx, dz)
            )
            c.start()
            cb1[(dx, dz)] = c
    bT[sq] = R1[x, zh]

    cu2 = spread(u1, cu, 1, U, u2s, u2r)
    for c in cu2:
        c.wait_recv()
    Uf[...] = jnp.dot(U[...].reshape(2048, 128), flip, preferred_element_type=f32)

    def lag_body(c, carry):
        gs = shifted(c)
        ut = Uf[pl.ds(c, 128, stride=16), :].T.astype(bf16)
        prev = None
        for e in range(8):
            m = jnp.dot(
                ut, jnp.concatenate([gs[2 * e], gs[2 * e + 1]], 1), preferred_element_type=f32
            )
            for d in (2 * e, 2 * e + 1):
                part = m[:, (d % 2) * 128:(d % 2) * 128 + 128]
                rolled = pltpu.roll(part, 1, 1, stride=1, stride_axis=0)
                if prev is not None:
                    Lp[pl.ds(pl.multiple_of(((d - 1) * 16 + c) * 8, 8), 8), :] = jnp.sum(
                        jnp.where(lower, prev, rolled).reshape(16, 8, 128), 0
                    )
                prev = rolled
        Lp[pl.ds(pl.multiple_of((15 * 16 + c) * 8, 8), 8), :] = jnp.sum(
            jnp.where(lower, prev, 0.0).reshape(16, 8, 128), 0
        )
        return carry
    lax.fori_loop(0, 16, lag_body, 0)

    lags = Lp[pl.ds(0, 256, stride=8), :]
    for k in range(1, 8):
        lags += Lp[pl.ds(k, 256, stride=8), :]
    L[...] = lags.reshape(16, 16, 128)

    clz = []
    for k in range(1, 4):
        c = remote(
            L.at[pl.ds(zl_index(k) * 4, 4)], LZ.at[k - 1],
            lzs.at[k - 1], lzr.at[k - 1], zl_dev(k),
        )
        c.start()
        clz.append(c)
    for c in clz:
        c.wait_recv()
    LS[...] = L[pl.ds(zl * 4, 4)] + LZ[0] + LZ[1] + LZ[2]
    clq = []
    for k in range(1, 8):
        c = remote(
            LS.at[q_index(k) // 2], LQ.at[q], lqs.at[k - 1], lqr.at[k - 1], q_dev(k)
        )
        c.start()
        clq.append(c)
    LQ[q] = LS[q // 2]
    for c in clq:
        c.wait_recv()
    table = LQ[...].reshape(128, 128).T
    of[...] = jnp.where(q % 2 == 0, table[:64], table[64:]) * (1.0 / 32.0)

    def finish(blk):
        cols = pl.ds(pl.multiple_of(blk * 128, 128), 128)
        back = bT[blk].astype(f32).T
        total = back + skip[:, cols] * gated(up, og, cols).astype(f32)
        oa[:, cols] = (total * sg[:, cols].astype(f32)).astype(bf16)
        ob[:, cols] = (total * ig[:, cols].astype(f32)).astype(bf16)

    for off in SEQ_OFFS:
        cb1[off].wait_recv()

    def ebody(k, carry):
        finish(k)
        return carry
    lax.fori_loop(0, 16, ebody, 0)

    for c in (
        list(cg.values()) + list(cu.values()) + ch + cg2 + cu2
        + [c for g in cb2 for c in g] + list(cb1.values()) + clz + clq
    ):
        c.wait_send()


def on_device(out_gate, in_gate, signal, upstream, filter_taps, skip_gain):
    vm = lambda shape, dtype: pltpu.VMEM(shape, dtype)
    dma = pltpu.SemaphoreType.DMA
    blocks = (16, 128, 128)
    quad = (4, 4, 128, 128)
    owned = (4, 4, 8, 16, 128)
    scratch = [
        vm(blocks, bf16), vm(blocks, bf16), vm(blocks, bf16),
        vm(quad, bf16), vm(quad, bf16),
        vm((16, 16, 128), bf16),
        vm(owned, bf16), vm(owned, bf16), vm(owned, bf16),
        vm(quad, bf16), vm(blocks, bf16),
        vm((2048, 128), f32), vm((2048, 128), f32), vm((2048, 128), f32),
        vm((256, 128), f32), vm((2048, 128), f32),
        vm((16, 16, 128), f32), vm((3, 4, 16, 128), f32),
        vm((4, 16, 128), f32), vm((8, 16, 128), f32),
    ]
    for shape in ((15,), (15,), (15,), (4, 7), (4, 7), (4, 7), (15,), (3,), (7,)):
        scratch += [dma(shape), dma(shape)]
    spec = pl.BlockSpec(memory_space=pltpu.VMEM)
    a, b, lag = pl.pallas_call(
        kernel,
        out_shape=(
            jax.ShapeDtypeStruct((128, 2048), bf16),
            jax.ShapeDtypeStruct((128, 2048), bf16),
            jax.ShapeDtypeStruct((64, 128), f32),
        ),
        in_specs=[spec] * 6,
        out_specs=(spec,) * 3,
        scratch_shapes=scratch,
        compiler_params=pltpu.CompilerParams(
            collective_id=0, has_side_effects=True, vmem_limit_bytes=40 * 1024 * 1024
        ),
    )(out_gate[0], in_gate[0], signal[0], upstream[0], filter_taps, skip_gain[None, :])
    return a[None], b[None], lag


def solution(mesh):
    return jax.shard_map(
        on_device,
        mesh=mesh,
        in_specs=(
            P("dp", "seq", None),
            P("dp", "seq", None),
            P("dp", "seq", None),
            P("dp", "seq", None),
            P("seq", None),
            P(),
        ),
        out_specs=(P("dp", "seq", None), P("dp", "seq", None), P("dp", "seq")),
        check_vma=False,
    )
```

```python
import jax
import jax.numpy as jnp
from jax import lax
from jax.experimental import pallas as pl
from jax.experimental.pallas import tpu as pltpu
from jax.sharding import PartitionSpec as P

MESH = pl.DeviceIdType.MESH
f32 = jnp.float32
bf16 = jnp.bfloat16

GROUPS = [[(dx, dz) for dz in (1, 3, 2, 0) if (dx, dz) != (0, 0)] for dx in range(4)]
SLOT = {off: i for i, off in enumerate(off for group in GROUPS for off in group)}


def kernel(
    og_hbm, ig_hbm, sg_hbm, up_hbm, ft_hbm, skip_hbm,
    oa, ob, of,
    og, ig, sg, up, ft, skip,
    gT, uT, hT, g1, u1, H, G, U, BC, R1, bT, Gf, Uf, Bf, HR, Lp, L, LZ, LS, LQ,
    ins, g1s, g1r, u1s, u1r, hs, hr, g2s, g2r, u2s, u2r, b2s, b2r, b1s, b1r, lzs, lzr, lqs, lqr,
):
    dp = lax.axis_index("dp")
    sq = lax.axis_index("seq")
    x, zh = sq // 4, sq % 4
    zl, q = dp // 8, dp % 8

    def seq_index(dx, dz, sign=1):
        return ((x + sign * dx + 4) % 4) * 4 + (zh + sign * dz + 4) % 4

    def seq_dev(dx, dz):
        return (dp, seq_index(dx, dz))

    def q_index(k):
        return (q + k) % 8

    def q_dev(k):
        return (zl * 8 + q_index(k), sq)

    def zl_index(k):
        return (zl + k) % 4

    def zl_dev(k):
        return (zl_index(k) * 8 + q, sq)

    def remote(src, dst, ssem, rsem, dev):
        return pltpu.make_async_remote_copy(
            src_ref=src, dst_ref=dst, send_sem=ssem, recv_sem=rsem,
            device_id=dev, device_id_type=MESH,
        )

    barrier = pltpu.get_barrier_semaphore()
    for group in GROUPS:
        for off in group:
            pl.semaphore_signal(barrier, inc=1, device_id=seq_dev(*off), device_id_type=MESH)
    for k in range(1, 8):
        pl.semaphore_signal(barrier, inc=1, device_id=q_dev(k), device_id_type=MESH)
    for k in range(1, 4):
        pl.semaphore_signal(barrier, inc=1, device_id=zl_dev(k), device_id_type=MESH)

    loads = [
        pltpu.make_async_copy(src, dst, ins.at[i])
        for i, (src, dst) in enumerate(
            [(up_hbm, up), (og_hbm, og), (ft_hbm, ft), (ig_hbm, ig), (sg_hbm, sg), (skip_hbm, skip)]
        )
    ]
    for c in loads:
        c.start()

    def gated(a_ref, b_ref, cols):
        return (a_ref[:, cols].astype(f32) * b_ref[:, cols].astype(f32)).astype(bf16)

    def prepare(a_ref, b_ref, out):
        def body(k, carry):
            cols = pl.ds(pl.multiple_of(k * 128, 128), 128)
            out[k] = gated(a_ref, b_ref, cols).astype(f32).T.astype(bf16)
            return carry
        lax.fori_loop(0, 16, body, 0)

    loads[0].wait()
    loads[1].wait()
    prepare(up, og, gT)

    pl.semaphore_wait(barrier, 25)

    def scatter(n, send, recv, ss, rs):
        copies = []
        for off in GROUPS[n]:
            i = SLOT[off]
            c = remote(send.at[seq_index(*off)], recv.at[x, zh], ss.at[i], rs.at[i], seq_dev(*off))
            c.start()
            copies.append(c)
        return copies

    def sent(copies):
        for c in copies:
            c.wait_send()

    def arrived(copies):
        for c in copies:
            c.wait_recv()

    mine = pl.ds(pl.multiple_of(q * 16, 16), 16)

    def spread(n, first, out, ss, rs):
        copies = []
        xs = (x - n + 4) % 4
        for k in range(1, 8):
            t = pl.ds(pl.multiple_of(q_index(k) * 16, 16), 16)
            c = remote(
                first.at[xs, :, t, :], out.at[xs, :, q],
                ss.at[n, k - 1], rs.at[n, k - 1], q_dev(k),
            )
            c.start()
            copies.append(c)
        out[xs, :, q] = first[xs, :, mine, :]
        return copies

    cg = [scatter(n, gT, g1, g1s, g1r) for n in range(3)]

    loads[2].wait()

    def hbody(k, carry):
        cols = pl.ds(pl.multiple_of(k * 128, 128), 128)
        hT[k] = ft[:, cols].astype(f32).T.astype(bf16)
        return carry
    lax.fori_loop(0, 16, hbody, 0)
    H[sq] = hT[sq, mine, :]
    g1[x, zh] = gT[sq]

    sent(cg[0])
    cg.append(scatter(3, gT, g1, g1s, g1r))
    loads[3].wait()
    loads[4].wait()
    prepare(ig, sg, uT)
    u1[x, zh] = uT[sq]

    cg2 = []
    arrived(cg[0])
    cg2.append(spread(0, g1, G, g2s, g2r))
    sent(cg[1])
    ch = []
    for group in GROUPS:
        for off in group:
            i = SLOT[off]
            c = remote(
                hT.at[seq_index(*off), mine], H.at[sq], hs.at[i], hr.at[i], seq_dev(*off)
            )
            c.start()
            ch.append(c)
    cu = [scatter(0, uT, u1, u1s, u1r)]
    arrived(cg[1])
    cg2.append(spread(1, g1, G, g2s, g2r))
    sent(cg[2])
    cu.append(scatter(1, uT, u1, u1s, u1r))
    arrived(cg[2])
    cg2.append(spread(2, g1, G, g2s, g2r))
    sent(cg[3])
    cu.append(scatter(2, uT, u1, u1s, u1r))
    arrived(cg[3])
    cg2.append(spread(3, g1, G, g2s, g2r))

    row = lax.broadcasted_iota(jnp.int32, (128, 128), 0)
    col = lax.broadcasted_iota(jnp.int32, (128, 128), 1)
    lower = col <= row
    flip = jnp.where(row + col == 127, 1.0, 0.0).astype(bf16)

    arrived(ch)
    HR[...] = jnp.dot(H[...].reshape(256, 128), flip, preferred_element_type=f32)
    sent(cu[0])
    cu.append(scatter(3, uT, u1, u1s, u1r))

    for group in cg2:
        arrived(group)
    Gf[...] = G[...].reshape(2048, 128).astype(f32)

    def shifted(c):
        rows = Gf[pl.ds(c, 128, stride=16), :]
        zero = jnp.zeros((128, 128), f32)
        even = jnp.concatenate([rows, zero], 0).astype(bf16)
        odd = jnp.concatenate([rows[8:], zero, zero[:8]], 0).astype(bf16)
        return [(even, odd)[d % 2][(d // 2) * 16:(d // 2) * 16 + 128] for d in range(16)]

    def conv_body(c, carry):
        gs = shifted(c)
        h = HR[pl.ds(c, 16, stride=16), :]
        prev = jnp.zeros((128, 128), f32)
        total = jnp.zeros((128, 128), f32)
        for e in range(8):
            ws = []
            for d in (2 * e, 2 * e + 1):
                rolled = pltpu.roll(
                    jnp.broadcast_to(h[d:d + 1], (128, 128)), 1, 1, stride=1, stride_axis=0
                )
                ws.append(jnp.where(lower, rolled, prev).astype(bf16))
                prev = rolled
            total += jnp.dot(
                jnp.concatenate([gs[2 * e], gs[2 * e + 1]], 1), jnp.concatenate(ws, 0),
                preferred_element_type=f32,
            )
        Bf[pl.ds(c, 128, stride=16), :] = total
        return carry
    lax.fori_loop(0, 16, conv_body, 0)
    BC[...] = Bf[...].astype(bf16).reshape(4, 4, 8, 16, 128)

    cb2 = []
    for n in range(4):
        xt = (x + n) % 4
        group = []
        for k in range(1, 8):
            c = remote(
                BC.at[xt, :, q_index(k)], R1.at[xt, :, mine, :],
                b2s.at[n, k - 1], b2r.at[n, k - 1], q_dev(k),
            )
            c.start()
            group.append(c)
        R1[xt, :, mine, :] = BC[xt, :, q]
        cb2.append(group)

    def send_back(n):
        arrived(cb2[n])
        copies = []
        for dx, dz in GROUPS[n]:
            i = SLOT[(dx, dz)]
            c = remote(
                R1.at[(x + dx) % 4, (zh + dz) % 4], bT.at[sq],
                b1s.at[i], b1r.at[i], seq_dev(dx, dz),
            )
            c.start()
            copies.append(c)
        return copies

    cu2 = []
    arrived(cu[0])
    cu2.append(spread(0, u1, U, u2s, u2r))
    cb1 = [send_back(0)]
    bT[sq] = R1[x, zh]
    arrived(cu[1])
    cu2.append(spread(1, u1, U, u2s, u2r))
    cb1.append(send_back(1))
    arrived(cu[2])
    cu2.append(spread(2, u1, U, u2s, u2r))
    cb1.append(send_back(2))
    cb1.append(send_back(3))
    arrived(cu[3])
    cu2.append(spread(3, u1, U, u2s, u2r))

    for group in cu2:
        arrived(group)
    Uf[...] = jnp.dot(U[...].reshape(2048, 128), flip, preferred_element_type=f32)

    def lag_body(c, carry):
        gs = shifted(c)
        ut = Uf[pl.ds(c, 128, stride=16), :].T.astype(bf16)
        prev = None
        for e in range(8):
            m = jnp.dot(
                ut, jnp.concatenate([gs[2 * e], gs[2 * e + 1]], 1), preferred_element_type=f32
            )
            for d in (2 * e, 2 * e + 1):
                part = m[:, (d % 2) * 128:(d % 2) * 128 + 128]
                rolled = pltpu.roll(part, 1, 1, stride=1, stride_axis=0)
                if prev is not None:
                    Lp[pl.ds(pl.multiple_of(((d - 1) * 16 + c) * 8, 8), 8), :] = jnp.sum(
                        jnp.where(lower, prev, rolled).reshape(16, 8, 128), 0
                    )
                prev = rolled
        Lp[pl.ds(pl.multiple_of((15 * 16 + c) * 8, 8), 8), :] = jnp.sum(
            jnp.where(lower, prev, 0.0).reshape(16, 8, 128), 0
        )
        return carry
    lax.fori_loop(0, 16, lag_body, 0)

    lags = Lp[pl.ds(0, 256, stride=8), :]
    for k in range(1, 8):
        lags += Lp[pl.ds(k, 256, stride=8), :]
    L[...] = lags.reshape(16, 16, 128)

    def finish(n):
        arrived(cb1[n])

        def body(j, carry):
            blk = ((x - n + 4) % 4) * 4 + j
            cols = pl.ds(pl.multiple_of(blk * 128, 128), 128)
            back = bT[blk].astype(f32).T
            total = back + skip[:, cols] * gated(up, og, cols).astype(f32)
            oa[:, cols] = (total * sg[:, cols].astype(f32)).astype(bf16)
            ob[:, cols] = (total * ig[:, cols].astype(f32)).astype(bf16)
            return carry
        lax.fori_loop(0, 4, body, 0)

    clz = []
    for k in range(1, 4):
        c = remote(
            L.at[pl.ds(zl_index(k) * 4, 4)], LZ.at[k - 1],
            lzs.at[k - 1], lzr.at[k - 1], zl_dev(k),
        )
        c.start()
        clz.append(c)
    loads[5].wait()
    finish(0)
    arrived(clz)
    LS[...] = L[pl.ds(zl * 4, 4)] + LZ[0] + LZ[1] + LZ[2]
    clq = []
    for k in range(1, 8):
        c = remote(
            LS.at[q_index(k) // 2], LQ.at[q], lqs.at[k - 1], lqr.at[k - 1], q_dev(k)
        )
        c.start()
        clq.append(c)
    LQ[q] = LS[q // 2]
    finish(1)
    arrived(clq)
    table = LQ[...].reshape(128, 128).T
    of[...] = jnp.where(q % 2 == 0, table[:64], table[64:]) * (1.0 / 32.0)
    finish(2)
    finish(3)

    for group in [cu[1], cu[2], cu[3], ch, clz, clq] + cg2 + cu2 + cb2 + cb1:
        sent(group)


def on_device(out_gate, in_gate, signal, upstream, filter_taps, skip_gain):
    vm = lambda shape, dtype: pltpu.VMEM(shape, dtype)
    dma = pltpu.SemaphoreType.DMA
    blocks = (16, 128, 128)
    quad = (4, 4, 128, 128)
    owned = (4, 4, 8, 16, 128)
    scratch = [vm((128, 2048), bf16)] * 5 + [vm((1, 2048), f32)] + [
        vm(blocks, bf16), vm(blocks, bf16), vm(blocks, bf16),
        vm(quad, bf16), vm(quad, bf16),
        vm((16, 16, 128), bf16),
        vm(owned, bf16), vm(owned, bf16), vm(owned, bf16),
        vm(quad, bf16), vm(blocks, bf16),
        vm((2048, 128), f32), vm((2048, 128), f32), vm((2048, 128), f32),
        vm((256, 128), f32), vm((2048, 128), f32),
        vm((16, 16, 128), f32), vm((3, 4, 16, 128), f32),
        vm((4, 16, 128), f32), vm((8, 16, 128), f32),
    ]
    scratch.append(dma((6,)))
    for shape in ((15,), (15,), (15,), (4, 7), (4, 7), (4, 7), (15,), (3,), (7,)):
        scratch += [dma(shape), dma(shape)]
    spec = pl.BlockSpec(memory_space=pltpu.VMEM)
    a, b, lag = pl.pallas_call(
        kernel,
        out_shape=(
            jax.ShapeDtypeStruct((128, 2048), bf16),
            jax.ShapeDtypeStruct((128, 2048), bf16),
            jax.ShapeDtypeStruct((64, 128), f32),
        ),
        in_specs=[pl.BlockSpec(memory_space=pltpu.HBM)] * 6,
        out_specs=(spec,) * 3,
        scratch_shapes=scratch,
        compiler_params=pltpu.CompilerParams(
            collective_id=0, has_side_effects=True, vmem_limit_bytes=56 * 1024 * 1024
        ),
    )(out_gate[0], in_gate[0], signal[0], upstream[0], filter_taps, skip_gain[None, :])
    return a[None], b[None], lag


def solution(mesh):
    return jax.shard_map(
        on_device,
        mesh=mesh,
        in_specs=(
            P("dp", "seq", None),
            P("dp", "seq", None),
            P("dp", "seq", None),
            P("dp", "seq", None),
            P("seq", None),
            P(),
        ),
        out_specs=(P("dp", "seq", None), P("dp", "seq", None), P("dp", "seq")),
        check_vma=False,
    )
```

```python
import jax
import jax.numpy as jnp
from jax import lax
from jax.experimental import pallas as pl
from jax.experimental.pallas import tpu as pltpu
from jax.sharding import PartitionSpec as P

MESH = pl.DeviceIdType.MESH
f32 = jnp.float32
bf16 = jnp.bfloat16

GROUPS = [[(dx, dz) for dz in (1, 3, 2, 0) if (dx, dz) != (0, 0)] for dx in range(4)]
SLOT = {off: i for i, off in enumerate(off for group in GROUPS for off in group)}


def kernel(
    og_hbm, ig_hbm, sg_hbm, up_hbm, ft_hbm, skip_hbm,
    oa, ob, of,
    og, ig, sg, up, ft, skip,
    gT, uT, hT, g1, u1, H, G, U, BC, R1, bT, Gf, Uf, Bf, HR, Lp, L, LZ, LS, LQ,
    ins, g1s, g1r, u1s, u1r, hs, hr, g2s, g2r, u2s, u2r, b2s, b2r, b1s, b1r, lzs, lzr, lqs, lqr,
):
    dp = lax.axis_index("dp")
    sq = lax.axis_index("seq")
    x, zh = sq // 4, sq % 4
    zl, q = dp // 8, dp % 8

    def seq_index(dx, dz, sign=1):
        return ((x + sign * dx + 4) % 4) * 4 + (zh + sign * dz + 4) % 4

    def seq_dev(dx, dz):
        return (dp, seq_index(dx, dz))

    def q_index(k):
        return (q + k) % 8

    def q_dev(k):
        return (zl * 8 + q_index(k), sq)

    def zl_index(k):
        return (zl + k) % 4

    def zl_dev(k):
        return (zl_index(k) * 8 + q, sq)

    def remote(src, dst, ssem, rsem, dev):
        return pltpu.make_async_remote_copy(
            src_ref=src, dst_ref=dst, send_sem=ssem, recv_sem=rsem,
            device_id=dev, device_id_type=MESH,
        )

    barrier = pltpu.get_barrier_semaphore()
    for group in GROUPS:
        for off in group:
            pl.semaphore_signal(barrier, inc=1, device_id=seq_dev(*off), device_id_type=MESH)
    for k in range(1, 8):
        pl.semaphore_signal(barrier, inc=1, device_id=q_dev(k), device_id_type=MESH)
    for k in range(1, 4):
        pl.semaphore_signal(barrier, inc=1, device_id=zl_dev(k), device_id_type=MESH)

    loads = [
        pltpu.make_async_copy(src, dst, ins.at[i])
        for i, (src, dst) in enumerate(
            [(up_hbm, up), (og_hbm, og), (ft_hbm, ft), (ig_hbm, ig), (sg_hbm, sg), (skip_hbm, skip)]
        )
    ]
    for c in loads:
        c.start()

    def gated(a_ref, b_ref, cols):
        return (a_ref[:, cols].astype(f32) * b_ref[:, cols].astype(f32)).astype(bf16)

    def prepare(a_ref, b_ref, out):
        def body(k, carry):
            cols = pl.ds(pl.multiple_of(k * 128, 128), 128)
            out[k] = gated(a_ref, b_ref, cols).astype(f32).T.astype(bf16)
            return carry
        lax.fori_loop(0, 16, body, 0)

    loads[0].wait()
    loads[1].wait()
    prepare(up, og, gT)

    pl.semaphore_wait(barrier, 25)

    def scatter(n, send, recv, ss, rs):
        copies = []
        for off in GROUPS[n]:
            i = SLOT[off]
            c = remote(send.at[seq_index(*off)], recv.at[x, zh], ss.at[i], rs.at[i], seq_dev(*off))
            c.start()
            copies.append(c)
        return copies

    def sent(copies):
        for c in copies:
            c.wait_send()

    def arrived(copies):
        for c in copies:
            c.wait_recv()

    mine = pl.ds(pl.multiple_of(q * 16, 16), 16)

    def spread(n, first, out, ss, rs):
        copies = []
        xs = (x - n + 4) % 4
        for k in range(1, 8):
            t = pl.ds(pl.multiple_of(q_index(k) * 16, 16), 16)
            c = remote(
                first.at[xs, :, t, :], out.at[xs, :, q],
                ss.at[n, k - 1], rs.at[n, k - 1], q_dev(k),
            )
            c.start()
            copies.append(c)
        out[xs, :, q] = first[xs, :, mine, :]
        return copies

    cg = [scatter(n, gT, g1, g1s, g1r) for n in range(3)]

    loads[2].wait()

    def hbody(k, carry):
        cols = pl.ds(pl.multiple_of(k * 128, 128), 128)
        hT[k] = ft[:, cols].astype(f32).T.astype(bf16)
        return carry
    lax.fori_loop(0, 16, hbody, 0)
    H[sq] = hT[sq, mine, :]

    def start_taps(i, src, dst, dev):
        c = remote(src, dst, hs.at[i], hr.at[i], dev)
        c.start()
        return c

    ch = []
    cz = []
    for d in range(1, 4):
        cz.append(
            start_taps(d + 2, hT.at[seq_index(zl, d), mine], H.at[sq], seq_dev(zl, d))
        )
    for d in range(1, 4):
        ch.append(start_taps(d - 1, hT.at[seq_index(d, 0), mine], H.at[sq], seq_dev(d, 0)))

    def share_taps():
        arrived(cz)
        for d in range(1, 4):
            tile = H.at[seq_index(zl, d, -1)]
            for k in range(1, 4):
                ch.append(start_taps(k * 3 + d + 2, tile, tile, zl_dev(k)))

    g1[x, zh] = gT[sq]

    sent(cg[0])
    cg.append(scatter(3, gT, g1, g1s, g1r))
    loads[3].wait()
    loads[4].wait()
    prepare(ig, sg, uT)
    u1[x, zh] = uT[sq]

    cg2 = []
    arrived(cg[0])
    cg2.append(spread(0, g1, G, g2s, g2r))
    sent(cg[1])
    cu = [scatter(0, uT, u1, u1s, u1r)]
    arrived(cg[1])
    cg2.append(spread(1, g1, G, g2s, g2r))
    share_taps()
    sent(cg[2])
    cu.append(scatter(1, uT, u1, u1s, u1r))
    arrived(cg[2])
    cg2.append(spread(2, g1, G, g2s, g2r))
    sent(cg[3])
    cu.append(scatter(2, uT, u1, u1s, u1r))
    arrived(cg[3])
    cg2.append(spread(3, g1, G, g2s, g2r))

    row = lax.broadcasted_iota(jnp.int32, (128, 128), 0)
    col = lax.broadcasted_iota(jnp.int32, (128, 128), 1)
    lower = col <= row
    flip = jnp.where(row + col == 127, 1.0, 0.0).astype(bf16)

    arrived(ch)
    HR[...] = jnp.dot(H[...].reshape(256, 128), flip, preferred_element_type=f32)
    sent(cu[0])
    cu.append(scatter(3, uT, u1, u1s, u1r))

    for group in cg2:
        arrived(group)
    Gf[...] = G[...].reshape(2048, 128).astype(f32)

    def shifted(c):
        rows = Gf[pl.ds(c, 128, stride=16), :]
        zero = jnp.zeros((128, 128), f32)
        even = jnp.concatenate([rows, zero], 0).astype(bf16)
        odd = jnp.concatenate([rows[8:], zero, zero[:8]], 0).astype(bf16)
        return [(even, odd)[d % 2][(d // 2) * 16:(d // 2) * 16 + 128] for d in range(16)]

    def conv_body(c, carry):
        gs = shifted(c)
        h = HR[pl.ds(c, 16, stride=16), :]
        prev = jnp.zeros((128, 128), f32)
        total = jnp.zeros((128, 128), f32)
        for e in range(8):
            ws = []
            for d in (2 * e, 2 * e + 1):
                rolled = pltpu.roll(
                    jnp.broadcast_to(h[d:d + 1], (128, 128)), 1, 1, stride=1, stride_axis=0
                )
                ws.append(jnp.where(lower, rolled, prev).astype(bf16))
                prev = rolled
            total += jnp.dot(
                jnp.concatenate([gs[2 * e], gs[2 * e + 1]], 1), jnp.concatenate(ws, 0),
                preferred_element_type=f32,
            )
        Bf[pl.ds(c, 128, stride=16), :] = total
        return carry
    lax.fori_loop(0, 16, conv_body, 0)
    BC[...] = Bf[...].astype(bf16).reshape(4, 4, 8, 16, 128)

    cb2 = []
    for n in range(4):
        xt = (x + n) % 4
        group = []
        for k in range(1, 8):
            c = remote(
                BC.at[xt, :, q_index(k)], R1.at[xt, :, mine, :],
                b2s.at[n, k - 1], b2r.at[n, k - 1], q_dev(k),
            )
            c.start()
            group.append(c)
        R1[xt, :, mine, :] = BC[xt, :, q]
        cb2.append(group)

    def send_back(n):
        arrived(cb2[n])
        copies = []
        for dx, dz in GROUPS[n]:
            i = SLOT[(dx, dz)]
            c = remote(
                R1.at[(x + dx) % 4, (zh + dz) % 4], bT.at[sq],
                b1s.at[i], b1r.at[i], seq_dev(dx, dz),
            )
            c.start()
            copies.append(c)
        return copies

    cu2 = []
    arrived(cu[0])
    cu2.append(spread(0, u1, U, u2s, u2r))
    cb1 = [send_back(0)]
    bT[sq] = R1[x, zh]
    arrived(cu[1])
    cu2.append(spread(1, u1, U, u2s, u2r))
    cb1.append(send_back(1))
    arrived(cu[2])
    cu2.append(spread(2, u1, U, u2s, u2r))
    cb1.append(send_back(2))
    cb1.append(send_back(3))
    arrived(cu[3])
    cu2.append(spread(3, u1, U, u2s, u2r))

    for group in cu2:
        arrived(group)
    Uf[...] = jnp.dot(U[...].reshape(2048, 128), flip, preferred_element_type=f32)

    def lag_body(c, carry):
        gs = shifted(c)
        ut = Uf[pl.ds(c, 128, stride=16), :].T.astype(bf16)
        prev = None
        for e in range(8):
            m = jnp.dot(
                ut, jnp.concatenate([gs[2 * e], gs[2 * e + 1]], 1), preferred_element_type=f32
            )
            for d in (2 * e, 2 * e + 1):
                part = m[:, (d % 2) * 128:(d % 2) * 128 + 128]
                rolled = pltpu.roll(part, 1, 1, stride=1, stride_axis=0)
                if prev is not None:
                    Lp[pl.ds(pl.multiple_of(((d - 1) * 16 + c) * 8, 8), 8), :] = jnp.sum(
                        jnp.where(lower, prev, rolled).reshape(16, 8, 128), 0
                    )
                prev = rolled
        Lp[pl.ds(pl.multiple_of((15 * 16 + c) * 8, 8), 8), :] = jnp.sum(
            jnp.where(lower, prev, 0.0).reshape(16, 8, 128), 0
        )
        return carry
    lax.fori_loop(0, 16, lag_body, 0)

    lags = Lp[pl.ds(0, 256, stride=8), :]
    for k in range(1, 8):
        lags += Lp[pl.ds(k, 256, stride=8), :]
    L[...] = lags.reshape(16, 16, 128)

    def finish(n):
        arrived(cb1[n])

        def body(j, carry):
            blk = ((x - n + 4) % 4) * 4 + j
            cols = pl.ds(pl.multiple_of(blk * 128, 128), 128)
            back = bT[blk].astype(f32).T
            total = back + skip[:, cols] * gated(up, og, cols).astype(f32)
            oa[:, cols] = (total * sg[:, cols].astype(f32)).astype(bf16)
            ob[:, cols] = (total * ig[:, cols].astype(f32)).astype(bf16)
            return carry
        lax.fori_loop(0, 4, body, 0)

    clz = []
    for k in range(1, 4):
        c = remote(
            L.at[pl.ds(zl_index(k) * 4, 4)], LZ.at[k - 1],
            lzs.at[k - 1], lzr.at[k - 1], zl_dev(k),
        )
        c.start()
        clz.append(c)
    loads[5].wait()
    finish(0)
    arrived(clz)
    LS[...] = L[pl.ds(zl * 4, 4)] + LZ[0] + LZ[1] + LZ[2]
    clq = []
    for k in range(1, 8):
        c = remote(
            LS.at[q_index(k) // 2], LQ.at[q], lqs.at[k - 1], lqr.at[k - 1], q_dev(k)
        )
        c.start()
        clq.append(c)
    LQ[q] = LS[q // 2]
    finish(1)
    arrived(clq)
    table = LQ[...].reshape(128, 128).T
    of[...] = jnp.where(q % 2 == 0, table[:64], table[64:]) * (1.0 / 32.0)
    finish(2)
    finish(3)

    for group in [cu[1], cu[2], cu[3], ch, cz, clz, clq] + cg2 + cu2 + cb2 + cb1:
        sent(group)


def on_device(out_gate, in_gate, signal, upstream, filter_taps, skip_gain):
    vm = lambda shape, dtype: pltpu.VMEM(shape, dtype)
    dma = pltpu.SemaphoreType.DMA
    blocks = (16, 128, 128)
    quad = (4, 4, 128, 128)
    owned = (4, 4, 8, 16, 128)
    scratch = [vm((128, 2048), bf16)] * 5 + [vm((1, 2048), f32)] + [
        vm(blocks, bf16), vm(blocks, bf16), vm(blocks, bf16),
        vm(quad, bf16), vm(quad, bf16),
        vm((16, 16, 128), bf16),
        vm(owned, bf16), vm(owned, bf16), vm(owned, bf16),
        vm(quad, bf16), vm(blocks, bf16),
        vm((2048, 128), f32), vm((2048, 128), f32), vm((2048, 128), f32),
        vm((256, 128), f32), vm((2048, 128), f32),
        vm((16, 16, 128), f32), vm((3, 4, 16, 128), f32),
        vm((4, 16, 128), f32), vm((8, 16, 128), f32),
    ]
    scratch.append(dma((6,)))
    for shape in ((15,), (15,), (15,), (4, 7), (4, 7), (4, 7), (15,), (3,), (7,)):
        scratch += [dma(shape), dma(shape)]
    spec = pl.BlockSpec(memory_space=pltpu.VMEM)
    a, b, lag = pl.pallas_call(
        kernel,
        out_shape=(
            jax.ShapeDtypeStruct((128, 2048), bf16),
            jax.ShapeDtypeStruct((128, 2048), bf16),
            jax.ShapeDtypeStruct((64, 128), f32),
        ),
        in_specs=[pl.BlockSpec(memory_space=pltpu.HBM)] * 6,
        out_specs=(spec,) * 3,
        scratch_shapes=scratch,
        compiler_params=pltpu.CompilerParams(
            collective_id=0, has_side_effects=True, vmem_limit_bytes=40 * 1024 * 1024
        ),
    )(out_gate[0], in_gate[0], signal[0], upstream[0], filter_taps, skip_gain[None, :])
    return a[None], b[None], lag


def solution(mesh):
    return jax.shard_map(
        on_device,
        mesh=mesh,
        in_specs=(
            P("dp", "seq", None),
            P("dp", "seq", None),
            P("dp", "seq", None),
            P("dp", "seq", None),
            P("seq", None),
            P(),
        ),
        out_specs=(P("dp", "seq", None), P("dp", "seq", None), P("dp", "seq")),
        check_vma=False,
    )
```

```python
import jax
import jax.numpy as jnp
from jax import lax
from jax.experimental import pallas as pl
from jax.experimental.pallas import tpu as pltpu
from jax.sharding import PartitionSpec as P

MESH = pl.DeviceIdType.MESH
f32 = jnp.float32
bf16 = jnp.bfloat16

GROUPS = [[(dx, dz) for dz in (1, 3, 2, 0) if (dx, dz) != (0, 0)] for dx in range(4)]
SLOT = {off: i for i, off in enumerate(off for group in GROUPS for off in group)}


def kernel(
    og_hbm, ig_hbm, sg_hbm, up_hbm, ft_hbm, skip_hbm,
    oa, ob, of,
    og, ig, sg, up, ft, skip,
    gT, uT, hT, g1, u1, H, G, U, BC, R1, bT, Gf, Uf, Bf, HR, Lp, L, LZ, LS, LQ,
    ins, g1s, g1r, u1s, u1r, hs, hr, g2s, g2r, u2s, u2r, b2s, b2r, b1s, b1r, lzs, lzr, lqs, lqr,
):
    dp = lax.axis_index("dp")
    sq = lax.axis_index("seq")
    x, zh = sq // 4, sq % 4
    zl, q = dp // 8, dp % 8

    def seq_index(dx, dz, sign=1):
        return ((x + sign * dx + 4) % 4) * 4 + (zh + sign * dz + 4) % 4

    def seq_dev(dx, dz):
        return (dp, seq_index(dx, dz))

    def q_index(k):
        return (q + k) % 8

    def q_dev(k):
        return (zl * 8 + q_index(k), sq)

    def zl_index(k):
        return (zl + k) % 4

    def zl_dev(k):
        return (zl_index(k) * 8 + q, sq)

    def remote(src, dst, ssem, rsem, dev):
        return pltpu.make_async_remote_copy(
            src_ref=src, dst_ref=dst, send_sem=ssem, recv_sem=rsem,
            device_id=dev, device_id_type=MESH,
        )

    barrier = pltpu.get_barrier_semaphore()
    for group in GROUPS:
        for off in group:
            pl.semaphore_signal(barrier, inc=1, device_id=seq_dev(*off), device_id_type=MESH)
    for k in range(1, 8):
        pl.semaphore_signal(barrier, inc=1, device_id=q_dev(k), device_id_type=MESH)
    for k in range(1, 4):
        pl.semaphore_signal(barrier, inc=1, device_id=zl_dev(k), device_id_type=MESH)

    loads = [
        pltpu.make_async_copy(src, dst, ins.at[i])
        for i, (src, dst) in enumerate(
            [(up_hbm, up), (og_hbm, og), (ft_hbm, ft), (ig_hbm, ig), (sg_hbm, sg), (skip_hbm, skip)]
        )
    ]
    for c in loads:
        c.start()

    def gated(a_ref, b_ref, cols):
        return (a_ref[:, cols].astype(f32) * b_ref[:, cols].astype(f32)).astype(bf16)

    def prepare(a_ref, b_ref, out):
        def body(k, carry):
            cols = pl.ds(pl.multiple_of(k * 128, 128), 128)
            out[k] = gated(a_ref, b_ref, cols).astype(f32).T.astype(bf16)
            return carry
        lax.fori_loop(0, 16, body, 0)

    loads[0].wait()
    loads[1].wait()
    prepare(up, og, gT)

    pl.semaphore_wait(barrier, 25)

    def scatter(n, send, recv, ss, rs):
        copies = []
        for off in GROUPS[n]:
            i = SLOT[off]
            c = remote(send.at[seq_index(*off)], recv.at[x, zh], ss.at[i], rs.at[i], seq_dev(*off))
            c.start()
            copies.append(c)
        return copies

    def sent(copies):
        for c in copies:
            c.wait_send()

    def arrived(copies):
        for c in copies:
            c.wait_recv()

    mine = pl.ds(pl.multiple_of(q * 16, 16), 16)

    def spread(n, first, out, ss, rs):
        copies = []
        xs = (x - n + 4) % 4
        for k in range(1, 8):
            t = pl.ds(pl.multiple_of(q_index(k) * 16, 16), 16)
            c = remote(
                first.at[xs, :, t, :], out.at[xs, :, q],
                ss.at[n, k - 1], rs.at[n, k - 1], q_dev(k),
            )
            c.start()
            copies.append(c)
        out[xs, :, q] = first[xs, :, mine, :]
        return copies

    cg = [scatter(n, gT, g1, g1s, g1r) for n in range(3)]

    loads[2].wait()

    def hbody(k, carry):
        cols = pl.ds(pl.multiple_of(k * 128, 128), 128)
        hT[k] = ft[:, cols].astype(f32).T.astype(bf16)
        return carry
    lax.fori_loop(0, 16, hbody, 0)
    H[sq] = hT[sq, mine, :]

    def start_taps(i, src, dst, dev):
        c = remote(src, dst, hs.at[i], hr.at[i], dev)
        c.start()
        return c

    ch = []
    cz = []
    for d in range(1, 4):
        cz.append(
            start_taps(d + 2, hT.at[seq_index(zl, d), mine], H.at[sq], seq_dev(zl, d))
        )
    for d in range(1, 4):
        ch.append(start_taps(d - 1, hT.at[seq_index(d, 0), mine], H.at[sq], seq_dev(d, 0)))

    def share_taps():
        arrived(cz)
        for d in range(1, 4):
            tile = H.at[seq_index(zl, d, -1)]
            for k in range(1, 4):
                ch.append(start_taps(k * 3 + d + 2, tile, tile, zl_dev(k)))

    g1[x, zh] = gT[sq]

    sent(cg[0])
    cg.append(scatter(3, gT, g1, g1s, g1r))
    loads[3].wait()
    loads[4].wait()
    prepare(ig, sg, uT)
    u1[x, zh] = uT[sq]

    cg2 = []
    arrived(cg[0])
    cg2.append(spread(0, g1, G, g2s, g2r))
    arrived(cg[1])
    cg2.append(spread(1, g1, G, g2s, g2r))
    share_taps()
    sent(cg[1])
    sent(cg[2])
    cu = [scatter(0, uT, u1, u1s, u1r)]
    arrived(cg[2])
    cg2.append(spread(2, g1, G, g2s, g2r))
    sent(cg[3])
    cu.append(scatter(1, uT, u1, u1s, u1r))
    cu.append(scatter(2, uT, u1, u1s, u1r))
    arrived(cg[3])
    cg2.append(spread(3, g1, G, g2s, g2r))

    row = lax.broadcasted_iota(jnp.int32, (128, 128), 0)
    col = lax.broadcasted_iota(jnp.int32, (128, 128), 1)
    lower = col <= row
    flip = jnp.where(row + col == 127, 1.0, 0.0).astype(bf16)

    arrived(ch)
    HR[...] = jnp.dot(H[...].reshape(256, 128), flip, preferred_element_type=f32)
    sent(cu[0])
    cu.append(scatter(3, uT, u1, u1s, u1r))

    for group in cg2:
        arrived(group)
    Gf[...] = G[...].reshape(2048, 128).astype(f32)

    def shifted(c):
        rows = Gf[pl.ds(c, 128, stride=16), :]
        zero = jnp.zeros((128, 128), f32)
        even = jnp.concatenate([rows, zero], 0).astype(bf16)
        odd = jnp.concatenate([rows[8:], zero, zero[:8]], 0).astype(bf16)
        return [(even, odd)[d % 2][(d // 2) * 16:(d // 2) * 16 + 128] for d in range(16)]

    def conv_body(c, carry):
        gs = shifted(c)
        h = HR[pl.ds(c, 16, stride=16), :]
        prev = jnp.zeros((128, 128), f32)
        total = jnp.zeros((128, 128), f32)
        for e in range(8):
            ws = []
            for d in (2 * e, 2 * e + 1):
                rolled = pltpu.roll(
                    jnp.broadcast_to(h[d:d + 1], (128, 128)), 1, 1, stride=1, stride_axis=0
                )
                ws.append(jnp.where(lower, rolled, prev).astype(bf16))
                prev = rolled
            total += jnp.dot(
                jnp.concatenate([gs[2 * e], gs[2 * e + 1]], 1), jnp.concatenate(ws, 0),
                preferred_element_type=f32,
            )
        Bf[pl.ds(c, 128, stride=16), :] = total
        return carry
    lax.fori_loop(0, 16, conv_body, 0)
    BC[...] = Bf[...].astype(bf16).reshape(4, 4, 8, 16, 128)

    cb2 = []

    def turn(n):
        xt = (x + n) % 4
        group = []
        for k in range(1, 8):
            c = remote(
                BC.at[xt, :, q_index(k)], R1.at[xt, :, mine, :],
                b2s.at[n, k - 1], b2r.at[n, k - 1], q_dev(k),
            )
            c.start()
            group.append(c)
        R1[xt, :, mine, :] = BC[xt, :, q]
        cb2.append(group)

    def send_back(n):
        arrived(cb2[n])
        copies = []
        for dx, dz in GROUPS[n]:
            i = SLOT[(dx, dz)]
            c = remote(
                R1.at[(x + dx) % 4, (zh + dz) % 4], bT.at[sq],
                b1s.at[i], b1r.at[i], seq_dev(dx, dz),
            )
            c.start()
            copies.append(c)
        return copies

    cu2 = []
    turn(0)
    turn(1)
    cb1 = [send_back(0)]
    bT[sq] = R1[x, zh]
    turn(2)
    cb1.append(send_back(1))
    turn(3)
    arrived(cu[0])
    cu2.append(spread(0, u1, U, u2s, u2r))
    arrived(cu[1])
    cu2.append(spread(1, u1, U, u2s, u2r))
    cb1.append(send_back(2))
    arrived(cu[2])
    cu2.append(spread(2, u1, U, u2s, u2r))
    cb1.append(send_back(3))
    arrived(cu[3])
    cu2.append(spread(3, u1, U, u2s, u2r))

    for group in cu2:
        arrived(group)
    Uf[...] = jnp.dot(U[...].reshape(2048, 128), flip, preferred_element_type=f32)

    def lag_body(c, carry):
        gs = shifted(c)
        ut = Uf[pl.ds(c, 128, stride=16), :].T.astype(bf16)
        prev = None
        for e in range(8):
            m = jnp.dot(
                ut, jnp.concatenate([gs[2 * e], gs[2 * e + 1]], 1), preferred_element_type=f32
            )
            for d in (2 * e, 2 * e + 1):
                part = m[:, (d % 2) * 128:(d % 2) * 128 + 128]
                rolled = pltpu.roll(part, 1, 1, stride=1, stride_axis=0)
                if prev is not None:
                    Lp[pl.ds(pl.multiple_of(((d - 1) * 16 + c) * 8, 8), 8), :] = jnp.sum(
                        jnp.where(lower, prev, rolled).reshape(16, 8, 128), 0
                    )
                prev = rolled
        Lp[pl.ds(pl.multiple_of((15 * 16 + c) * 8, 8), 8), :] = jnp.sum(
            jnp.where(lower, prev, 0.0).reshape(16, 8, 128), 0
        )
        return carry
    lax.fori_loop(0, 16, lag_body, 0)

    lags = Lp[pl.ds(0, 256, stride=8), :]
    for k in range(1, 8):
        lags += Lp[pl.ds(k, 256, stride=8), :]
    L[...] = lags.reshape(16, 16, 128)

    def finish(n):
        arrived(cb1[n])

        def body(j, carry):
            blk = ((x - n + 4) % 4) * 4 + j
            cols = pl.ds(pl.multiple_of(blk * 128, 128), 128)
            back = bT[blk].astype(f32).T
            total = back + skip[:, cols] * gated(up, og, cols).astype(f32)
            oa[:, cols] = (total * sg[:, cols].astype(f32)).astype(bf16)
            ob[:, cols] = (total * ig[:, cols].astype(f32)).astype(bf16)
            return carry
        lax.fori_loop(0, 4, body, 0)

    clz = []
    for k in range(1, 4):
        c = remote(
            L.at[pl.ds(zl_index(k) * 4, 4)], LZ.at[k - 1],
            lzs.at[k - 1], lzr.at[k - 1], zl_dev(k),
        )
        c.start()
        clz.append(c)
    loads[5].wait()
    finish(0)
    arrived(clz)
    LS[...] = L[pl.ds(zl * 4, 4)] + LZ[0] + LZ[1] + LZ[2]
    clq = []
    for k in range(1, 8):
        c = remote(
            LS.at[q_index(k) // 2], LQ.at[q], lqs.at[k - 1], lqr.at[k - 1], q_dev(k)
        )
        c.start()
        clq.append(c)
    LQ[q] = LS[q // 2]
    finish(1)
    arrived(clq)
    table = LQ[...].reshape(128, 128).T
    of[...] = jnp.where(q % 2 == 0, table[:64], table[64:]) * (1.0 / 32.0)
    finish(2)
    finish(3)

    for group in [cu[1], cu[2], cu[3], ch, cz, clz, clq] + cg2 + cu2 + cb2 + cb1:
        sent(group)


def on_device(out_gate, in_gate, signal, upstream, filter_taps, skip_gain):
    vm = lambda shape, dtype: pltpu.VMEM(shape, dtype)
    dma = pltpu.SemaphoreType.DMA
    blocks = (16, 128, 128)
    quad = (4, 4, 128, 128)
    owned = (4, 4, 8, 16, 128)
    scratch = [vm((128, 2048), bf16)] * 5 + [vm((1, 2048), f32)] + [
        vm(blocks, bf16), vm(blocks, bf16), vm(blocks, bf16),
        vm(quad, bf16), vm(quad, bf16),
        vm((16, 16, 128), bf16),
        vm(owned, bf16), vm(owned, bf16), vm(owned, bf16),
        vm(quad, bf16), vm(blocks, bf16),
        vm((2048, 128), f32), vm((2048, 128), f32), vm((2048, 128), f32),
        vm((256, 128), f32), vm((2048, 128), f32),
        vm((16, 16, 128), f32), vm((3, 4, 16, 128), f32),
        vm((4, 16, 128), f32), vm((8, 16, 128), f32),
    ]
    scratch.append(dma((6,)))
    for shape in ((15,), (15,), (15,), (4, 7), (4, 7), (4, 7), (15,), (3,), (7,)):
        scratch += [dma(shape), dma(shape)]
    spec = pl.BlockSpec(memory_space=pltpu.VMEM)
    a, b, lag = pl.pallas_call(
        kernel,
        out_shape=(
            jax.ShapeDtypeStruct((128, 2048), bf16),
            jax.ShapeDtypeStruct((128, 2048), bf16),
            jax.ShapeDtypeStruct((64, 128), f32),
        ),
        in_specs=[pl.BlockSpec(memory_space=pltpu.HBM)] * 6,
        out_specs=(spec,) * 3,
        scratch_shapes=scratch,
        compiler_params=pltpu.CompilerParams(
            collective_id=0, has_side_effects=True, vmem_limit_bytes=56 * 1024 * 1024
        ),
    )(out_gate[0], in_gate[0], signal[0], upstream[0], filter_taps, skip_gain[None, :])
    return a[None], b[None], lag


def solution(mesh):
    return jax.shard_map(
        on_device,
        mesh=mesh,
        in_specs=(
            P("dp", "seq", None),
            P("dp", "seq", None),
            P("dp", "seq", None),
            P("dp", "seq", None),
            P("seq", None),
            P(),
        ),
        out_specs=(P("dp", "seq", None), P("dp", "seq", None), P("dp", "seq")),
        check_vma=False,
    )
```

```python
import jax
import jax.numpy as jnp
from jax import lax
from jax.experimental import pallas as pl
from jax.experimental.pallas import tpu as pltpu
from jax.sharding import PartitionSpec as P

MESH = pl.DeviceIdType.MESH
f32 = jnp.float32
bf16 = jnp.bfloat16

GROUPS = [[(dx, dz) for dz in (2, 1, 3, 0) if (dx, dz) != (0, 0)] for dx in range(4)]
SLOT = {off: i for i, off in enumerate(off for group in GROUPS for off in group)}


def kernel(
    og_hbm, ig_hbm, sg_hbm, up_hbm, ft_hbm, skip_hbm,
    oa, ob, of,
    og, ig, sg, up, ft, skip,
    gT, uT, hT, g1, u1, H, G, U, BC, R1, bT, Gf, Uf, Bf, HR, Lp, L, LZ, LS, LQ,
    ins, g1s, g1r, u1s, u1r, hs, hr, g2s, g2r, u2s, u2r, b2s, b2r, b1s, b1r, lzs, lzr, lqs, lqr,
):
    dp = lax.axis_index("dp")
    sq = lax.axis_index("seq")
    x, zh = sq // 4, sq % 4
    zl, q = dp // 8, dp % 8

    def seq_index(dx, dz, sign=1):
        return ((x + sign * dx + 4) % 4) * 4 + (zh + sign * dz + 4) % 4

    def seq_dev(dx, dz):
        return (dp, seq_index(dx, dz))

    def q_index(k):
        return (q + k) % 8

    def q_dev(k):
        return (zl * 8 + q_index(k), sq)

    def zl_index(k):
        return (zl + k) % 4

    def zl_dev(k):
        return (zl_index(k) * 8 + q, sq)

    def remote(src, dst, ssem, rsem, dev):
        return pltpu.make_async_remote_copy(
            src_ref=src, dst_ref=dst, send_sem=ssem, recv_sem=rsem,
            device_id=dev, device_id_type=MESH,
        )

    barrier = pltpu.get_barrier_semaphore()
    for group in GROUPS:
        for off in group:
            pl.semaphore_signal(barrier, inc=1, device_id=seq_dev(*off), device_id_type=MESH)
    for k in range(1, 8):
        pl.semaphore_signal(barrier, inc=1, device_id=q_dev(k), device_id_type=MESH)
    for k in range(1, 4):
        pl.semaphore_signal(barrier, inc=1, device_id=zl_dev(k), device_id_type=MESH)

    loads = [
        pltpu.make_async_copy(src, dst, ins.at[i])
        for i, (src, dst) in enumerate(
            [(up_hbm, up), (og_hbm, og), (ft_hbm, ft), (ig_hbm, ig), (sg_hbm, sg), (skip_hbm, skip)]
        )
    ]
    for c in loads:
        c.start()

    def gated(a_ref, b_ref, cols):
        return (a_ref[:, cols].astype(f32) * b_ref[:, cols].astype(f32)).astype(bf16)

    def prepare(a_ref, b_ref, out):
        def body(k, carry):
            cols = pl.ds(pl.multiple_of(k * 128, 128), 128)
            out[k] = gated(a_ref, b_ref, cols).astype(f32).T.astype(bf16)
            return carry
        lax.fori_loop(0, 16, body, 0)

    loads[0].wait()
    loads[1].wait()
    prepare(up, og, gT)

    pl.semaphore_wait(barrier, 25)

    def scatter(n, send, recv, ss, rs):
        copies = []
        for off in GROUPS[n]:
            i = SLOT[off]
            c = remote(send.at[seq_index(*off)], recv.at[x, zh], ss.at[i], rs.at[i], seq_dev(*off))
            c.start()
            copies.append(c)
        return copies

    def sent(copies):
        for c in copies:
            c.wait_send()

    def arrived(copies):
        for c in copies:
            c.wait_recv()

    mine = pl.ds(pl.multiple_of(q * 16, 16), 16)

    def spread(n, first, out, ss, rs):
        copies = []
        xs = (x - n + 4) % 4
        for k in range(1, 8):
            t = pl.ds(pl.multiple_of(q_index(k) * 16, 16), 16)
            c = remote(
                first.at[xs, :, t, :], out.at[xs, :, q],
                ss.at[n, k - 1], rs.at[n, k - 1], q_dev(k),
            )
            c.start()
            copies.append(c)
        out[xs, :, q] = first[xs, :, mine, :]
        return copies

    cg = [scatter(n, gT, g1, g1s, g1r) for n in range(3)]

    loads[2].wait()

    def hbody(k, carry):
        cols = pl.ds(pl.multiple_of(k * 128, 128), 128)
        hT[k] = ft[:, cols].astype(f32).T.astype(bf16)
        return carry
    lax.fori_loop(0, 16, hbody, 0)
    H[sq] = hT[sq, mine, :]

    def start_taps(i, src, dst, dev):
        c = remote(src, dst, hs.at[i], hr.at[i], dev)
        c.start()
        return c

    ch = []
    cz = []
    for d in range(1, 4):
        cz.append(
            start_taps(d + 2, hT.at[seq_index(zl, d), mine], H.at[sq], seq_dev(zl, d))
        )
    for d in range(1, 4):
        ch.append(start_taps(d - 1, hT.at[seq_index(d, 0), mine], H.at[sq], seq_dev(d, 0)))

    def share_taps():
        arrived(cz)
        for d in range(1, 4):
            tile = H.at[seq_index(zl, d, -1)]
            for k in range(1, 4):
                ch.append(start_taps(k * 3 + d + 2, tile, tile, zl_dev(k)))

    g1[x, zh] = gT[sq]

    sent(cg[0])
    cg.append(scatter(3, gT, g1, g1s, g1r))
    loads[3].wait()
    loads[4].wait()
    prepare(ig, sg, uT)
    u1[x, zh] = uT[sq]

    cg2 = []
    arrived(cg[0])
    cg2.append(spread(0, g1, G, g2s, g2r))
    arrived(cg[1])
    cg2.append(spread(1, g1, G, g2s, g2r))
    share_taps()
    sent(cg[1])
    sent(cg[2])
    cu = [scatter(0, uT, u1, u1s, u1r)]
    arrived(cg[2])
    cg2.append(spread(2, g1, G, g2s, g2r))
    sent(cg[3])
    cu.append(scatter(1, uT, u1, u1s, u1r))
    cu.append(scatter(2, uT, u1, u1s, u1r))
    arrived(cg[3])
    cg2.append(spread(3, g1, G, g2s, g2r))

    row = lax.broadcasted_iota(jnp.int32, (128, 128), 0)
    col = lax.broadcasted_iota(jnp.int32, (128, 128), 1)
    lower = col <= row
    flip = jnp.where(row + col == 127, 1.0, 0.0).astype(bf16)

    arrived(ch)
    HR[...] = jnp.dot(H[...].reshape(256, 128), flip, preferred_element_type=f32)
    sent(cu[0])
    cu.append(scatter(3, uT, u1, u1s, u1r))

    for group in cg2:
        arrived(group)
    Gf[...] = G[...].reshape(2048, 128).astype(f32)

    def shifted(c):
        rows = Gf[pl.ds(c, 128, stride=16), :]
        zero = jnp.zeros((128, 128), f32)
        even = jnp.concatenate([rows, zero], 0).astype(bf16)
        odd = jnp.concatenate([rows[8:], zero, zero[:8]], 0).astype(bf16)
        return [(even, odd)[d % 2][(d // 2) * 16:(d // 2) * 16 + 128] for d in range(16)]

    def conv_body(c, carry):
        gs = shifted(c)
        h = HR[pl.ds(c, 16, stride=16), :]
        prev = jnp.zeros((128, 128), f32)
        total = jnp.zeros((128, 128), f32)
        for e in range(8):
            ws = []
            for d in (2 * e, 2 * e + 1):
                rolled = pltpu.roll(
                    jnp.broadcast_to(h[d:d + 1], (128, 128)), 1, 1, stride=1, stride_axis=0
                )
                ws.append(jnp.where(lower, rolled, prev).astype(bf16))
                prev = rolled
            total += jnp.dot(
                jnp.concatenate([gs[2 * e], gs[2 * e + 1]], 1), jnp.concatenate(ws, 0),
                preferred_element_type=f32,
            )
        Bf[pl.ds(c, 128, stride=16), :] = total
        return carry
    lax.fori_loop(0, 16, conv_body, 0)
    BC[...] = Bf[...].astype(bf16).reshape(4, 4, 8, 16, 128)

    cb2 = []

    def turn(n):
        xt = (x + n) % 4
        group = []
        for k in range(1, 8):
            c = remote(
                BC.at[xt, :, q_index(k)], R1.at[xt, :, mine, :],
                b2s.at[n, k - 1], b2r.at[n, k - 1], q_dev(k),
            )
            c.start()
            group.append(c)
        R1[xt, :, mine, :] = BC[xt, :, q]
        cb2.append(group)

    def send_back(n):
        arrived(cb2[n])
        copies = []
        for dx, dz in GROUPS[n]:
            i = SLOT[(dx, dz)]
            c = remote(
                R1.at[(x + dx) % 4, (zh + dz) % 4], bT.at[sq],
                b1s.at[i], b1r.at[i], seq_dev(dx, dz),
            )
            c.start()
            copies.append(c)
        return copies

    cu2 = []
    turn(0)
    turn(1)
    cb1 = [send_back(0)]
    bT[sq] = R1[x, zh]
    turn(2)
    cb1.append(send_back(1))
    turn(3)
    arrived(cu[0])
    cu2.append(spread(0, u1, U, u2s, u2r))
    arrived(cu[1])
    cu2.append(spread(1, u1, U, u2s, u2r))
    cb1.append(send_back(2))
    arrived(cu[2])
    cu2.append(spread(2, u1, U, u2s, u2r))
    cb1.append(send_back(3))
    arrived(cu[3])
    cu2.append(spread(3, u1, U, u2s, u2r))

    for group in cu2:
        arrived(group)
    Uf[...] = jnp.dot(U[...].reshape(2048, 128), flip, preferred_element_type=f32)

    def lag_body(c, carry):
        gs = shifted(c)
        ut = Uf[pl.ds(c, 128, stride=16), :].T.astype(bf16)
        prev = None
        for e in range(8):
            m = jnp.dot(
                ut, jnp.concatenate([gs[2 * e], gs[2 * e + 1]], 1), preferred_element_type=f32
            )
            for d in (2 * e, 2 * e + 1):
                part = m[:, (d % 2) * 128:(d % 2) * 128 + 128]
                rolled = pltpu.roll(part, 1, 1, stride=1, stride_axis=0)
                if prev is not None:
                    Lp[pl.ds(pl.multiple_of(((d - 1) * 16 + c) * 8, 8), 8), :] = jnp.sum(
                        jnp.where(lower, prev, rolled).reshape(16, 8, 128), 0
                    )
                prev = rolled
        Lp[pl.ds(pl.multiple_of((15 * 16 + c) * 8, 8), 8), :] = jnp.sum(
            jnp.where(lower, prev, 0.0).reshape(16, 8, 128), 0
        )
        return carry
    lax.fori_loop(0, 16, lag_body, 0)

    lags = Lp[pl.ds(0, 256, stride=8), :]
    for k in range(1, 8):
        lags += Lp[pl.ds(k, 256, stride=8), :]
    L[...] = lags.reshape(16, 16, 128)

    def finish(n):
        arrived(cb1[n])

        def body(j, carry):
            blk = ((x - n + 4) % 4) * 4 + j
            cols = pl.ds(pl.multiple_of(blk * 128, 128), 128)
            back = bT[blk].astype(f32).T
            total = back + skip[:, cols] * gated(up, og, cols).astype(f32)
            oa[:, cols] = (total * sg[:, cols].astype(f32)).astype(bf16)
            ob[:, cols] = (total * ig[:, cols].astype(f32)).astype(bf16)
            return carry
        lax.fori_loop(0, 4, body, 0)

    clz = []
    for k in range(1, 4):
        c = remote(
            L.at[pl.ds(zl_index(k) * 4, 4)], LZ.at[k - 1],
            lzs.at[k - 1], lzr.at[k - 1], zl_dev(k),
        )
        c.start()
        clz.append(c)
    loads[5].wait()
    finish(0)
    arrived(clz)
    LS[...] = L[pl.ds(zl * 4, 4)] + LZ[0] + LZ[1] + LZ[2]
    clq = []
    for k in range(1, 8):
        c = remote(
            LS.at[q_index(k) // 2], LQ.at[q], lqs.at[k - 1], lqr.at[k - 1], q_dev(k)
        )
        c.start()
        clq.append(c)
    LQ[q] = LS[q // 2]
    finish(1)
    arrived(clq)
    table = LQ[...].reshape(128, 128).T
    of[...] = jnp.where(q % 2 == 0, table[:64], table[64:]) * (1.0 / 32.0)
    finish(2)
    finish(3)

    for group in [cu[1], cu[2], cu[3], ch, cz, clz, clq] + cg2 + cu2 + cb2 + cb1:
        sent(group)


def on_device(out_gate, in_gate, signal, upstream, filter_taps, skip_gain):
    vm = lambda shape, dtype: pltpu.VMEM(shape, dtype)
    dma = pltpu.SemaphoreType.DMA
    blocks = (16, 128, 128)
    quad = (4, 4, 128, 128)
    owned = (4, 4, 8, 16, 128)
    scratch = [vm((128, 2048), bf16)] * 5 + [vm((1, 2048), f32)] + [
        vm(blocks, bf16), vm(blocks, bf16), vm(blocks, bf16),
        vm(quad, bf16), vm(quad, bf16),
        vm((16, 16, 128), bf16),
        vm(owned, bf16), vm(owned, bf16), vm(owned, bf16),
        vm(quad, bf16), vm(blocks, bf16),
        vm((2048, 128), f32), vm((2048, 128), f32), vm((2048, 128), f32),
        vm((256, 128), f32), vm((2048, 128), f32),
        vm((16, 16, 128), f32), vm((3, 4, 16, 128), f32),
        vm((4, 16, 128), f32), vm((8, 16, 128), f32),
    ]
    scratch.append(dma((6,)))
    for shape in ((15,), (15,), (15,), (4, 7), (4, 7), (4, 7), (15,), (3,), (7,)):
        scratch += [dma(shape), dma(shape)]
    spec = pl.BlockSpec(memory_space=pltpu.VMEM)
    a, b, lag = pl.pallas_call(
        kernel,
        out_shape=(
            jax.ShapeDtypeStruct((128, 2048), bf16),
            jax.ShapeDtypeStruct((128, 2048), bf16),
            jax.ShapeDtypeStruct((64, 128), f32),
        ),
        in_specs=[pl.BlockSpec(memory_space=pltpu.HBM)] * 6,
        out_specs=(spec,) * 3,
        scratch_shapes=scratch,
        compiler_params=pltpu.CompilerParams(
            collective_id=0, has_side_effects=True, vmem_limit_bytes=56 * 1024 * 1024
        ),
    )(out_gate[0], in_gate[0], signal[0], upstream[0], filter_taps, skip_gain[None, :])
    return a[None], b[None], lag


def solution(mesh):
    return jax.shard_map(
        on_device,
        mesh=mesh,
        in_specs=(
            P("dp", "seq", None),
            P("dp", "seq", None),
            P("dp", "seq", None),
            P("dp", "seq", None),
            P("seq", None),
            P(),
        ),
        out_specs=(P("dp", "seq", None), P("dp", "seq", None), P("dp", "seq")),
        check_vma=False,
    )
```

```python
import jax
import jax.numpy as jnp
from jax import lax
from jax.experimental import pallas as pl
from jax.experimental.pallas import tpu as pltpu
from jax.sharding import PartitionSpec as P

MESH = pl.DeviceIdType.MESH
f32 = jnp.float32
bf16 = jnp.bfloat16

GROUPS = [[(dx, dz) for dz in (2, 1, 3, 0) if (dx, dz) != (0, 0)] for dx in range(4)]
SLOT = {off: i for i, off in enumerate(off for group in GROUPS for off in group)}


def kernel(
    og_hbm, ig_hbm, sg_hbm, up_hbm, ft_hbm, skip_hbm,
    oa, ob, of,
    og, ig, sg, up, ft, skip,
    gT, uT, hT, g1, u1, H, G, U, BC, R1, bT, Gf, Uf, Bf, HR, Lp, L, LZ, LS, LQ,
    ins, g1s, g1r, u1s, u1r, hs, hr, g2s, g2r, u2s, u2r, b2s, b2r, b1s, b1r, lzs, lzr, lqs, lqr,
):
    dp = lax.axis_index("dp")
    sq = lax.axis_index("seq")
    x, zh = sq // 4, sq % 4
    zl, q = dp // 8, dp % 8

    def seq_index(dx, dz, sign=1):
        return ((x + sign * dx + 4) % 4) * 4 + (zh + sign * dz + 4) % 4

    def seq_dev(dx, dz):
        return (dp, seq_index(dx, dz))

    def q_index(k):
        return (q + k) % 8

    def q_dev(k):
        return (zl * 8 + q_index(k), sq)

    def zl_index(k):
        return (zl + k) % 4

    def zl_dev(k):
        return (zl_index(k) * 8 + q, sq)

    def remote(src, dst, ssem, rsem, dev):
        return pltpu.make_async_remote_copy(
            src_ref=src, dst_ref=dst, send_sem=ssem, recv_sem=rsem,
            device_id=dev, device_id_type=MESH,
        )

    barrier = pltpu.get_barrier_semaphore()
    for group in GROUPS:
        for off in group:
            pl.semaphore_signal(barrier, inc=1, device_id=seq_dev(*off), device_id_type=MESH)
    for k in range(1, 8):
        pl.semaphore_signal(barrier, inc=1, device_id=q_dev(k), device_id_type=MESH)
    for k in range(1, 4):
        pl.semaphore_signal(barrier, inc=1, device_id=zl_dev(k), device_id_type=MESH)

    loads = [
        pltpu.make_async_copy(src, dst, ins.at[i])
        for i, (src, dst) in enumerate(
            [(up_hbm, up), (og_hbm, og), (ft_hbm, ft), (ig_hbm, ig), (sg_hbm, sg), (skip_hbm, skip)]
        )
    ]
    for c in loads:
        c.start()

    def gated(a_ref, b_ref, cols):
        return (a_ref[:, cols].astype(f32) * b_ref[:, cols].astype(f32)).astype(bf16)

    def prepare(a_ref, b_ref, out):
        def body(k, carry):
            cols = pl.ds(pl.multiple_of(k * 128, 128), 128)
            out[k] = gated(a_ref, b_ref, cols).astype(f32).T.astype(bf16)
            return carry
        lax.fori_loop(0, 16, body, 0)

    loads[0].wait()
    loads[1].wait()
    prepare(up, og, gT)

    pl.semaphore_wait(barrier, 25)

    def scatter(n, send, recv, ss, rs):
        copies = []
        for off in GROUPS[n]:
            i = SLOT[off]
            c = remote(send.at[seq_index(*off)], recv.at[x, zh], ss.at[i], rs.at[i], seq_dev(*off))
            c.start()
            copies.append(c)
        return copies

    def sent(copies):
        for c in copies:
            c.wait_send()

    def arrived(copies):
        for c in copies:
            c.wait_recv()

    mine = pl.ds(pl.multiple_of(q * 16, 16), 16)

    def spread(n, first, out, ss, rs):
        copies = []
        xs = (x - n + 4) % 4
        for k in range(1, 8):
            t = pl.ds(pl.multiple_of(q_index(k) * 16, 16), 16)
            c = remote(
                first.at[xs, :, t, :], out.at[xs, :, q],
                ss.at[n, k - 1], rs.at[n, k - 1], q_dev(k),
            )
            c.start()
            copies.append(c)
        out[xs, :, q] = first[xs, :, mine, :]
        return copies

    cg = [scatter(n, gT, g1, g1s, g1r) for n in range(3)]

    loads[2].wait()

    def hbody(k, carry):
        cols = pl.ds(pl.multiple_of(k * 128, 128), 128)
        hT[k] = ft[:, cols].astype(f32).T.astype(bf16)
        return carry
    lax.fori_loop(0, 16, hbody, 0)
    H[sq] = hT[sq, mine, :]

    def start_taps(i, src, dst, dev):
        c = remote(src, dst, hs.at[i], hr.at[i], dev)
        c.start()
        return c

    ch = []
    cz = []
    for d in range(1, 4):
        cz.append(
            start_taps(d + 2, hT.at[seq_index(zl, d), mine], H.at[sq], seq_dev(zl, d))
        )
    for d in range(1, 4):
        ch.append(start_taps(d - 1, hT.at[seq_index(d, 0), mine], H.at[sq], seq_dev(d, 0)))

    def share_taps():
        arrived(cz)
        for d in range(1, 4):
            tile = H.at[seq_index(zl, d, -1)]
            for k in range(1, 4):
                ch.append(start_taps(k * 3 + d + 2, tile, tile, zl_dev(k)))

    g1[x, zh] = gT[sq]

    sent(cg[0])
    cg.append(scatter(3, gT, g1, g1s, g1r))
    loads[3].wait()
    loads[4].wait()
    prepare(ig, sg, uT)
    u1[x, zh] = uT[sq]

    cg2 = []
    arrived(cg[0])
    cg2.append(spread(0, g1, G, g2s, g2r))
    arrived(cg[1])
    cg2.append(spread(1, g1, G, g2s, g2r))
    share_taps()
    sent(cg[1])
    sent(cg[2])
    cu = [scatter(0, uT, u1, u1s, u1r)]
    arrived(cg[2])
    cg2.append(spread(2, g1, G, g2s, g2r))
    sent(cg[3])
    cu.append(scatter(1, uT, u1, u1s, u1r))
    cu.append(scatter(2, uT, u1, u1s, u1r))
    arrived(cg[3])
    cg2.append(spread(3, g1, G, g2s, g2r))

    row = lax.broadcasted_iota(jnp.int32, (128, 128), 0)
    col = lax.broadcasted_iota(jnp.int32, (128, 128), 1)
    lower = col <= row
    flip = jnp.where(row + col == 127, 1.0, 0.0).astype(bf16)

    arrived(ch)
    HR[...] = jnp.dot(H[...].reshape(256, 128), flip, preferred_element_type=f32)
    sent(cu[0])
    cu.append(scatter(3, uT, u1, u1s, u1r))

    for group in cg2:
        arrived(group)
    Gf[...] = G[...].reshape(2048, 128).astype(f32)

    def shifted(c):
        rows = Gf[pl.ds(c, 128, stride=16), :]
        zero = jnp.zeros((128, 128), f32)
        even = jnp.concatenate([rows, zero], 0).astype(bf16)
        odd = jnp.concatenate([rows[8:], zero, zero[:8]], 0).astype(bf16)
        return [(even, odd)[d % 2][(d // 2) * 16:(d // 2) * 16 + 128] for d in range(16)]

    def conv_body(c, carry):
        gs = shifted(c)
        h = HR[pl.ds(c, 16, stride=16), :]
        prev = jnp.zeros((128, 128), f32)
        total = jnp.zeros((128, 128), f32)
        for e in range(8):
            ws = []
            for d in (2 * e, 2 * e + 1):
                rolled = pltpu.roll(
                    jnp.broadcast_to(h[d:d + 1], (128, 128)), 1, 1, stride=1, stride_axis=0
                )
                ws.append(jnp.where(lower, rolled, prev).astype(bf16))
                prev = rolled
            total += jnp.dot(
                jnp.concatenate([gs[2 * e], gs[2 * e + 1]], 1), jnp.concatenate(ws, 0),
                preferred_element_type=f32,
            )
        Bf[pl.ds(c, 128, stride=16), :] = total
        return carry
    lax.fori_loop(0, 16, conv_body, 0)
    BC[...] = Bf[...].astype(bf16).reshape(4, 4, 8, 16, 128)

    cb2 = []

    def turn(n):
        xt = (x + n) % 4
        group = []
        for k in range(1, 8):
            c = remote(
                BC.at[xt, :, q_index(k)], R1.at[xt, :, mine, :],
                b2s.at[n, k - 1], b2r.at[n, k - 1], q_dev(k),
            )
            c.start()
            group.append(c)
        R1[xt, :, mine, :] = BC[xt, :, q]
        cb2.append(group)

    def send_back(n):
        arrived(cb2[n])
        copies = []
        for dx, dz in GROUPS[n]:
            i = SLOT[(dx, dz)]
            c = remote(
                R1.at[(x + dx) % 4, (zh + dz) % 4], bT.at[sq],
                b1s.at[i], b1r.at[i], seq_dev(dx, dz),
            )
            c.start()
            copies.append(c)
        return copies

    cu2 = []
    turn(0)
    turn(1)
    cb1 = [send_back(0)]
    bT[sq] = R1[x, zh]
    turn(2)
    cb1.append(send_back(1))
    turn(3)
    cb1.append(send_back(2))
    cb1.append(send_back(3))
    for n in range(4):
        arrived(cu[n])
        cu2.append(spread(n, u1, U, u2s, u2r))

    for group in cu2:
        arrived(group)
    Uf[...] = jnp.dot(U[...].reshape(2048, 128), flip, preferred_element_type=f32)

    def lag_body(c, carry):
        gs = shifted(c)
        ut = Uf[pl.ds(c, 128, stride=16), :].T.astype(bf16)
        prev = None
        for e in range(8):
            m = jnp.dot(
                ut, jnp.concatenate([gs[2 * e], gs[2 * e + 1]], 1), preferred_element_type=f32
            )
            for d in (2 * e, 2 * e + 1):
                part = m[:, (d % 2) * 128:(d % 2) * 128 + 128]
                rolled = pltpu.roll(part, 1, 1, stride=1, stride_axis=0)
                if prev is not None:
                    Lp[pl.ds(pl.multiple_of(((d - 1) * 16 + c) * 8, 8), 8), :] = jnp.sum(
                        jnp.where(lower, prev, rolled).reshape(16, 8, 128), 0
                    )
                prev = rolled
        Lp[pl.ds(pl.multiple_of((15 * 16 + c) * 8, 8), 8), :] = jnp.sum(
            jnp.where(lower, prev, 0.0).reshape(16, 8, 128), 0
        )
        return carry
    lax.fori_loop(0, 16, lag_body, 0)

    lags = Lp[pl.ds(0, 256, stride=8), :]
    for k in range(1, 8):
        lags += Lp[pl.ds(k, 256, stride=8), :]
    L[...] = lags.reshape(16, 16, 128)

    def finish(n):
        arrived(cb1[n])

        def body(j, carry):
            blk = ((x - n + 4) % 4) * 4 + j
            cols = pl.ds(pl.multiple_of(blk * 128, 128), 128)
            back = bT[blk].astype(f32).T
            total = back + skip[:, cols] * gated(up, og, cols).astype(f32)
            oa[:, cols] = (total * sg[:, cols].astype(f32)).astype(bf16)
            ob[:, cols] = (total * ig[:, cols].astype(f32)).astype(bf16)
            return carry
        lax.fori_loop(0, 4, body, 0)

    clz = []
    for k in range(1, 4):
        c = remote(
            L.at[pl.ds(zl_index(k) * 4, 4)], LZ.at[k - 1],
            lzs.at[k - 1], lzr.at[k - 1], zl_dev(k),
        )
        c.start()
        clz.append(c)
    loads[5].wait()
    finish(0)
    arrived(clz)
    LS[...] = L[pl.ds(zl * 4, 4)] + LZ[0] + LZ[1] + LZ[2]
    clq = []
    for k in range(1, 8):
        c = remote(
            LS.at[q_index(k) // 2], LQ.at[q], lqs.at[k - 1], lqr.at[k - 1], q_dev(k)
        )
        c.start()
        clq.append(c)
    LQ[q] = LS[q // 2]
    finish(1)
    arrived(clq)
    table = LQ[...].reshape(128, 128).T
    of[...] = jnp.where(q % 2 == 0, table[:64], table[64:]) * (1.0 / 32.0)
    finish(2)
    finish(3)

    for group in [cu[1], cu[2], cu[3], ch, cz, clz, clq] + cg2 + cu2 + cb2 + cb1:
        sent(group)


def on_device(out_gate, in_gate, signal, upstream, filter_taps, skip_gain):
    vm = lambda shape, dtype: pltpu.VMEM(shape, dtype)
    dma = pltpu.SemaphoreType.DMA
    blocks = (16, 128, 128)
    quad = (4, 4, 128, 128)
    owned = (4, 4, 8, 16, 128)
    scratch = [vm((128, 2048), bf16)] * 5 + [vm((1, 2048), f32)] + [
        vm(blocks, bf16), vm(blocks, bf16), vm(blocks, bf16),
        vm(quad, bf16), vm(quad, bf16),
        vm((16, 16, 128), bf16),
        vm(owned, bf16), vm(owned, bf16), vm(owned, bf16),
        vm(quad, bf16), vm(blocks, bf16),
        vm((2048, 128), f32), vm((2048, 128), f32), vm((2048, 128), f32),
        vm((256, 128), f32), vm((2048, 128), f32),
        vm((16, 16, 128), f32), vm((3, 4, 16, 128), f32),
        vm((4, 16, 128), f32), vm((8, 16, 128), f32),
    ]
    scratch.append(dma((6,)))
    for shape in ((15,), (15,), (15,), (4, 7), (4, 7), (4, 7), (15,), (3,), (7,)):
        scratch += [dma(shape), dma(shape)]
    spec = pl.BlockSpec(memory_space=pltpu.VMEM)
    a, b, lag = pl.pallas_call(
        kernel,
        out_shape=(
            jax.ShapeDtypeStruct((128, 2048), bf16),
            jax.ShapeDtypeStruct((128, 2048), bf16),
            jax.ShapeDtypeStruct((64, 128), f32),
        ),
        in_specs=[pl.BlockSpec(memory_space=pltpu.HBM)] * 6,
        out_specs=(spec,) * 3,
        scratch_shapes=scratch,
        compiler_params=pltpu.CompilerParams(
            collective_id=0, has_side_effects=True, vmem_limit_bytes=56 * 1024 * 1024
        ),
    )(out_gate[0], in_gate[0], signal[0], upstream[0], filter_taps, skip_gain[None, :])
    return a[None], b[None], lag


def solution(mesh):
    return jax.shard_map(
        on_device,
        mesh=mesh,
        in_specs=(
            P("dp", "seq", None),
            P("dp", "seq", None),
            P("dp", "seq", None),
            P("dp", "seq", None),
            P("seq", None),
            P(),
        ),
        out_specs=(P("dp", "seq", None), P("dp", "seq", None), P("dp", "seq")),
        check_vma=False,
    )
```
